32 devices in a mesh: row: 4 (over z), col: 8 (over y, x, core).
Axes of the slice: x: 2, y: 2, z: 4, core: 2. Of those that a mesh axis runs over, the one named last changes fastest.
Arguments:
- trailing: float32 [16384, 16384], P('row', 'col'), as said below
- cross: float32 [1024, 16384], P(('row', 'col')), may hold values from -6 to 6
Outputs:
- factored: float32 [16384, 16384], P('row', 'col')
- solved: float32 [1024, 16384], P('row', 'col')
The draws below stay inside these ranges and needn't reach their ends.
Inputs may be any that keep to these rules, and one draw needn't show every extreme that they name: trailing is symmetric and positive definite.
All inputs are finite; a program needn't handle non-finite values.
Results may differ from the reference program's by a relative error of at most 0.00025.
Values sent between devices are 32-bit elements; how exact they have to be, the bound alone decides.
A program may use at most 192 MiB of HBM per device.

```python
import jax
import jax.numpy as jnp
from jax import lax

M = 16384
B = 256
Q = 1024
TILE_ROWS = 16
TILE_COLS = 8
N_ROW = 4
N_COL = 8


def draw_trailing(key, part):
    tiles = M // B
    span_rows = tiles // TILE_ROWS
    span_cols = tiles // TILE_COLS
    first_key, second_key, scale_key = jax.random.split(jax.random.fold_in(key, 11), 3)
    first_points = jax.random.uniform(first_key, (2, M), jnp.float32)
    second_points = jax.random.uniform(second_key, (2, M), jnp.float32)
    first_length = 0.3
    second_length = 0.3
    weight = jnp.exp(jax.random.uniform(scale_key, (M,), jnp.float32, -0.5, 0.5))
    places = jnp.arange(M, dtype=jnp.int32)
    blocks = places // B
    inner = places % B
    row_nat = (blocks % TILE_ROWS * span_rows + blocks // TILE_ROWS) * B + inner
    col_nat = (blocks % TILE_COLS * span_cols + blocks // TILE_COLS) * B + inner

    def kernel(points, length):
        gap_x = points[0][row_nat][:, None] - points[0][col_nat][None, :]
        gap_y = points[1][row_nat][:, None] - points[1][col_nat][None, :]
        return jnp.exp(-jnp.sqrt(gap_x * gap_x + gap_y * gap_y) / length)
    same = (row_nat[:, None] == col_nat[None, :]).astype(jnp.float32)
    scales = weight[row_nat][:, None] * weight[col_nat][None, :]
    return 3.0 * scales * kernel(first_points, first_length) * kernel(second_points, second_length) + same


def shard_levels(stream_key, shape, cuts, low, largest):
    level = 1.0
    for axis_at, shards_of in cuts:
        steps = jax.random.uniform(jax.random.fold_in(jax.random.fold_in(stream_key, 6), axis_at), (shards_of,), jnp.float32, low / len(cuts), largest / len(cuts))
        level = level * jnp.repeat(jnp.exp(steps), shape[axis_at] // shards_of).reshape((-1,) + (1,) * (len(shape) - 1 - axis_at))
    return level


def noise(rng, shape, scale, bound, shards=(), held_as=jnp.bfloat16):
    values = scale * jax.random.normal(rng, shape, jnp.float32)
    if shards:
        values = values * shard_levels(rng, shape, shards, -0.22, 0.18)
    return jnp.clip(values, -bound, bound).astype(held_as)


def setup_inputs(seed: int = 0) -> dict:
    key_of = jax.random.split(jax.random.key(seed), 3)
    return {
        "trailing": draw_trailing(jax.random.fold_in(key_of[2], 71), 0),
        "cross": noise(key_of[1], (Q, M), 1.0, 6.0, ((0, 32),), jnp.float32),
    }


def stored_maps():
    places = jnp.arange(M, dtype=jnp.int32)
    blocks = places // B
    inner = places % B
    row_tile = blocks % TILE_ROWS * N_ROW + blocks // TILE_ROWS
    col_tile = blocks % TILE_COLS * N_COL + blocks // TILE_COLS
    return (row_tile, col_tile, inner)

def reference(trailing, cross):
    row_tile, col_tile, inner = stored_maps()
    exact = lax.Precision.HIGHEST
    tiles = M // B
    answer = cross[:, col_tile * B + inner]
    state = trailing
    place_of = (col_tile % N_ROW * TILE_ROWS + col_tile // N_ROW) * B + inner
    for panel in range(2):
        row_block = panel % N_ROW * TILE_ROWS + panel // N_ROW
        col_block = panel % N_COL * TILE_COLS + panel // N_COL
        slab = state[:, col_block * B:(col_block + 1) * B]
        factor = jnp.linalg.cholesky(slab[row_block * B:(row_block + 1) * B])
        scaled = lax.linalg.triangular_solve(factor, slab, left_side=False, lower=True, transpose_a=True)
        column = jnp.where((row_tile > panel)[:, None], scaled, 0.0)
        column = column.at[row_block * B:(row_block + 1) * B].set(factor)
        mirror = jnp.where((col_tile > panel)[:, None], column[place_of], 0.0)
        left_part = jnp.where((row_tile > panel)[:, None], column, 0.0)

        def lower_rows(pair):
            return pair[0] - jnp.dot(pair[1].astype(jnp.float32), mirror.T.astype(jnp.float32), precision=exact, preferred_element_type=jnp.float32)
        state = lax.map(lower_rows, (state.reshape(tiles, B, M), left_part.reshape(tiles, B, B))).reshape(M, M)
        state = state.at[:, col_block * B:(col_block + 1) * B].set(column)
        band = state[row_block * B:(row_block + 1) * B]
        state = state.at[row_block * B:(row_block + 1) * B].set(jnp.where((col_tile > panel)[None, :], 0.0, band))
        target = answer[:, col_block * B:(col_block + 1) * B]
        result = lax.linalg.triangular_solve(factor, target, left_side=False, lower=True, transpose_a=True)
        answer = answer - jnp.dot(result.astype(jnp.float32), mirror.T.astype(jnp.float32), precision=exact, preferred_element_type=jnp.float32)
        answer = answer.at[:, col_block * B:(col_block + 1) * B].set(result)
    return (state, answer)
```

```python
import functools

import jax
import jax.numpy as jnp
from jax import lax
from jax.experimental import pallas as pl
from jax.experimental.pallas import tpu as pltpu
from jax.sharding import PartitionSpec as P

B = 256
K2 = 2 * B
H = 128
MESH = pl.DeviceIdType.MESH
EXACT = lax.Precision.HIGHEST


def exact_dot(a, b, dims):
    return lax.dot_general(a, b, (dims, ((), ())), precision=EXACT, preferred_element_type=jnp.float32)


def eliminate(t, carry, g_ref):
    g = g_ref[...]
    row = g_ref[pl.ds(t, 1), :]
    lane = lax.broadcasted_iota(jnp.int32, (H, H), 1)
    sub = lax.broadcasted_iota(jnp.int32, (H, 1), 0)
    lane_row = lax.broadcasted_iota(jnp.int32, (1, H), 1)
    col = jnp.sum(jnp.where(lane == t, g[:, :H], 0.0), axis=1, keepdims=True)
    pivot = jnp.sum(jnp.where(lane_row == t, row[:, :H], 0.0), axis=1, keepdims=True)
    scaled = row * (1.0 / pivot)
    g_ref[...] = g - jnp.where(sub > t, col, 0.0) * scaled
    return carry


def factor_step(step, w_ref, e_ref, g_ref):
    j = step // 2
    half = step % 2
    at = pl.multiple_of(j * H, H)
    eye = lax.broadcasted_iota(jnp.int32, (H, H), 0) == lax.broadcasted_iota(jnp.int32, (H, H), 1)

    @pl.when(half == 0)
    def _():
        g_ref[:, :H] = w_ref[pl.ds(at, H), pl.ds(at, H)]
        g_ref[:, H:] = jnp.where(eye, 1.0, 0.0)

    lax.fori_loop(half * (H // 2), half * (H // 2) + H // 2, functools.partial(eliminate, g_ref=g_ref), 0)

    @pl.when(half == 1)
    def _():
        g = g_ref[...]
        diag = jnp.sum(jnp.where(eye, g[:, :H], 0.0), axis=1, keepdims=True)
        inv = g[:, H:] * (1.0 / jnp.sqrt(diag))
        rw = exact_dot(inv, w_ref[pl.ds(at, H), :], ((1,), (0,)))
        re = exact_dot(inv, e_ref[pl.ds(at, H), :], ((1,), (0,)))
        lane = lax.broadcasted_iota(jnp.int32, (H, K2), 1)
        rm = jnp.transpose(jnp.where(lane >= (j + 1) * H, rw, 0.0))
        w_ref[...] -= exact_dot(rm, rw, ((1,), (0,)))
        e_ref[...] -= exact_dot(rm, re, ((1,), (0,)))
        e_ref[pl.ds(at, H), :] = re


def exchange(
    R, C, tr, cross, pan, q, linv, ans, tq,
    w_ref, g_ref, zs, zb, zr, ps, pr, ss, sr, loc, xs, xr, ts, trv,
):
    m, n = tr.shape
    fq = cross.shape[0]
    nb = n // B
    npl = 1 + m // K2
    N = C // 2
    r = lax.axis_index("row")
    c = lax.axis_index("col")
    k = c % 2
    chip = c // 2
    y = chip // 2
    p = jnp.where(chip % 2 == 0, (N - y) % N, y + 1)

    def chip_at(pos):
        return jnp.where(pos > N // 2, 2 * (N - pos), jnp.maximum(2 * pos - 1, 0))

    nxt = [2 * chip_at((p + 1) % N) + k, 2 * chip_at((p + N - 1) % N) + k]
    last = [p == N - 1, p == 1]
    sib = c + 1 - 2 * k
    half_rows = m // 2

    own_q = [pltpu.make_async_copy(tr.at[pl.ds(0, B), :], q.at[pl.ds(t * B, B), :], loc.at[t]) for t in range(2)]
    own_p = [
        pltpu.make_async_copy(
            tr.at[pl.ds(d * half_rows, half_rows), pl.ds(0, B)],
            pan.at[k, d, pl.ds(B, half_rows), :],
            loc.at[2 + d],
        )
        for d in range(2)
    ]
    own_t = pltpu.make_async_copy(cross.at[:, pl.ds(0, K2)], tq.at[pl.ds(c * fq, fq), :], loc.at[4])

    def own_x(b):
        src = pl.multiple_of((b * C + c) * B, B)
        return pltpu.make_async_copy(
            cross.at[:, pl.ds(src, B)], ans.at[pl.ds(c * fq, fq), pl.ds(b * B, B)], loc.at[5 + b]
        )

    for t in range(2):
        @pl.when(r == t)
        def _():
            own_q[t].start()

        @pl.when(p == 0)
        def _():
            own_p[t].start()

    own_t.start()
    for b in range(nb):
        own_x(b).start()

    barrier = pltpu.get_barrier_semaphore()
    for o in range(1, C):
        pl.semaphore_signal(barrier, inc=1, device_id=(r, (c + o) % C), device_id_type=MESH)

    for o in (1, R - 1):
        pl.semaphore_signal(barrier, inc=1, device_id=((r + o) % R, c), device_id_type=MESH)
    pl.semaphore_wait(barrier, C + 1)

    for t in range(2):
        @pl.when(r == t)
        def _():
            own_q[t].wait()

        @pl.when(p == 0)
        def _():
            own_p[t].wait()

    def z_copy(t, b, down):
        piece = q.at[pl.ds(t * B, B), pl.ds(pl.multiple_of(b * B, B), B)]
        to = jnp.maximum(r - 1, 0) if down else jnp.minimum(r + 1, R - 1)
        return pltpu.make_async_remote_copy(
            piece, piece, zb.at[b] if down else zs.at[t, b], zr.at[t, b], device_id=(to, c), device_id_type=MESH
        )

    def p_copy(d, i):
        piece = pan.at[k, d, pl.ds(pl.multiple_of(i * B, B), B), :]
        return pltpu.make_async_remote_copy(
            piece, piece, ps.at[d, i], pr.at[d, i], device_id=(r, nxt[d]), device_id_type=MESH
        )

    def s_copy(d, i, core):
        piece = pan.at[core, d, pl.ds(pl.multiple_of(i * B, B), B), :]
        return pltpu.make_async_remote_copy(
            piece, piece, ss.at[d, i], sr.at[d, i], device_id=(r, sib), device_id_type=MESH
        )

    def x_copy(o, b):
        peer = (c + o) % C
        src = pl.multiple_of((b * C + peer) * B, B)
        return pltpu.make_async_remote_copy(
            cross.at[:, pl.ds(src, B)],
            ans.at[pl.ds(c * fq, fq), pl.ds(pl.multiple_of(b * B, B), B)],
            xs.at[o, b], xr.at[o, b], device_id=(r, peer), device_id_type=MESH,
        )

    def t_copy(o):
        return pltpu.make_async_remote_copy(
            cross.at[:, pl.ds(0, K2)], tq.at[pl.ds(c * fq, fq), :],
            ts.at[o], trv.at[o], device_id=(r, (c + o) % C), device_id_type=MESH,
        )

    def guarded(i, count, work):
        @pl.when(jnp.logical_and(i >= 0, i < count))
        def _():
            work(i)

    def z_pass(t, i):
        z_copy(t, i, False).wait_recv()

        @pl.when(jnp.logical_and(r > t, r < R - 1))
        def _():
            z_copy(t, i, False).start()

    def z_send(b, carry):
        for t in range(2):
            @pl.when(r == t)
            def _():
                z_copy(t, b, False).start()

        @pl.when(r == 1)
        def _():
            z_copy(1, b, True).start()

        return carry

    def z_item(step):
        for t in range(2):
            @pl.when(r != t)
            def _():
                lag = jnp.where(r > t, r - t - 1, 0)
                guarded(step - lag - 1, nb - 1, lambda i, t=t: z_pass(t, i + 1))

    def p_pass(d, i):
        @pl.when(p != 0)
        def _():
            p_copy(d, i).wait_recv()

            @pl.when(jnp.logical_not(last[d]))
            def _():
                p_copy(d, i).start()

        s_copy(d, i, k).start()

    def p_item(step):
        for d in range(2):
            hops = p if d == 0 else N - p
            lag = jnp.where(p == 0, 0, hops - 1)
            i = step - lag
            guarded(i - 1, npl - 1, lambda i, d=d: p_pass(d, i + 1))

    lax.fori_loop(0, nb, z_send, 0)
    for t in range(2):
        @pl.when(r != t)
        def _():
            z_pass(t, 0)

    @pl.when(p == 0)
    def _():
        for d in range(2):
            pltpu.make_async_copy(
                q.at[pl.ds(d * B, B), pl.ds(0, B)], pan.at[k, d, pl.ds(0, B), :], loc.at[d]
            ).start()
        for d in range(2):
            pltpu.make_async_copy(
                q.at[pl.ds(d * B, B), pl.ds(0, B)], pan.at[k, d, pl.ds(0, B), :], loc.at[d]
            ).wait()

    @pl.when(p == 0)
    def _():
        for d in range(2):
            p_copy(d, 0).start()

        def p_send(i, carry):
            for d in range(2):
                p_copy(d, i).start()
            return carry

        lax.fori_loop(1, npl, p_send, 0)

    def first(d):
        p_pass(d, 0)

    @pl.when(p <= N // 2)
    def _():
        first(0)
        first(1)

    @pl.when(p > N // 2)
    def _():
        first(1)
        first(0)

    for o in range(1, C):
        t_copy(o).start()
    for d in range(2):
        s_copy(d, 0, 1 - k).wait_recv()
    loads = [
        pltpu.make_async_copy(
            pan.at[core, d, pl.ds(0, B), :], w_ref.at[pl.ds(d * B, B), pl.ds(core * B, B)], loc.at[2 * core + d]
        )
        for core in range(2)
        for d in range(2)
    ]
    for load in loads:
        load.start()
    own_sub = lax.broadcasted_iota(jnp.int32, (K2, K2), 0)
    own_lane = lax.broadcasted_iota(jnp.int32, (K2, K2), 1)
    linv[...] = jnp.where(own_sub == own_lane, 1.0, 0.0)
    for load in loads:
        load.wait()

    steps = 2 * (K2 // H)

    def body(s, carry):
        z_item(s)
        p_item(s)

        @pl.when(s <= nb)
        def _():
            for o in range(1, C):
                x_copy(o, s - 1).start()

        @pl.when(s <= steps)
        def _():
            factor_step(s - 1, w_ref, linv, g_ref)

        return carry

    lax.fori_loop(1, max(nb + R, npl + N, steps) + 1, body, 0)

    own_t.wait()
    for b in range(nb):
        own_x(b).wait()

    def drain_z(b, carry):
        for t in range(2):
            @pl.when(jnp.logical_and(r >= t, r < R - 1))
            def _():
                z_copy(t, b, False).wait_send()

        @pl.when(r == 1)
        def _():
            z_copy(1, b, True).wait_send()

        for o in range(1, C):
            x_copy(o, b).wait_send()
            peer = (c + C - o) % C
            pltpu.make_async_remote_copy(
                cross.at[:, pl.ds(0, B)],
                ans.at[pl.ds(peer * fq, fq), pl.ds(pl.multiple_of(b * B, B), B)],
                xs.at[o, b], xr.at[o, b], device_id=(r, peer), device_id_type=MESH,
            ).wait_recv()
        return carry

    lax.fori_loop(0, nb, drain_z, 0)

    def drain_p(i, carry):
        for d in range(2):
            @pl.when(jnp.logical_not(last[d]))
            def _():
                p_copy(d, i).wait_send()

            s_copy(d, i, k).wait_send()

            @pl.when(i > 0)
            def _():
                s_copy(d, i, 1 - k).wait_recv()
        return carry

    lax.fori_loop(0, npl, drain_p, 0)
    for o in range(1, C):
        t_copy(o).wait_send()
        peer = (c + C - o) % C
        pltpu.make_async_remote_copy(
            cross.at[:, pl.ds(0, K2)], tq.at[pl.ds(peer * fq, fq), :],
            ts.at[o], trv.at[o], device_id=(r, peer), device_id_type=MESH,
        ).wait_recv()


def split(x):
    hi = x.astype(jnp.bfloat16)
    return hi, (x - hi.astype(jnp.float32)).astype(jnp.bfloat16)


def solve_rows(x0, x1, linv):
    c0 = exact_dot(x0, linv[:B, :B], ((1,), (1,)))
    c1 = exact_dot(x0, linv[B:, :B], ((1,), (1,))) + exact_dot(x1, linv[B:, B:], ((1,), (1,)))
    return c0, c1


def update(R, C, pan, q, linv, tr, ans, tq, out, sol, hi_ref, lo_ref):
    i = pl.program_id(0)
    r = lax.axis_index("row")
    c = lax.axis_index("col")
    n = q.shape[1]
    width = min(n, 512)

    def product(hi, lo, cols):
        dot = functools.partial(jnp.dot, preferred_element_type=jnp.float32)
        mh = hi_ref[:, cols]
        return dot(hi, mh) + dot(hi, lo_ref[:, cols]) + dot(lo, mh)

    @pl.when(i == 0)
    def _():
        for a in range(0, n, width):
            cols = slice(a, a + width)
            q0 = q[:B, cols]
            m0 = exact_dot(linv[:B, :B], q0, ((1,), (0,)))
            m1 = exact_dot(linv[B:, :B], q0, ((1,), (0,))) + exact_dot(linv[B:, B:], q[B:, cols], ((1,), (0,)))
            hi_ref[:B, cols], lo_ref[:B, cols] = split(m0)
            hi_ref[B:, cols], lo_ref[B:, cols] = split(m1)
        y0, y1 = solve_rows(tq[:, :B], tq[:, B:], linv)
        hi, lo = split(jnp.concatenate([y0, y1], axis=1))
        for a in range(0, n, width):
            cols = slice(a, a + width)
            sol[:, cols] = ans[:, cols] - product(hi, lo, cols)

        @pl.when(c == 0)
        def _():
            sol[:, :B] = y0

        @pl.when(c == 1)
        def _():
            sol[:, :B] = y1

    tile = i * R + r
    c0, c1 = solve_rows(pan[0, 0], pan[1, 0], linv)
    low = lax.broadcasted_iota(jnp.int32, (B, B), 0) >= lax.broadcasted_iota(jnp.int32, (B, B), 1)
    c0 = jnp.where(jnp.logical_or(tile > 0, low), c0, 0.0)
    c1 = jnp.where(jnp.logical_or(tile > 1, jnp.logical_and(low, tile == 1)), c1, 0.0)

    @pl.when(tile <= 1)
    def _():
        out[...] = jnp.zeros_like(out)

    @pl.when(tile > 1)
    def _():
        hi, lo = split(jnp.concatenate([c0, c1], axis=1))
        for a in range(0, n, width):
            cols = slice(a, a + width)
            out[:, cols] = tr[:, cols] - product(hi, lo, cols)

    @pl.when(c == 0)
    def _():
        out[:, :B] = c0

    @pl.when(c == 1)
    def _():
        out[:, :B] = c1


def on_device(R, C, trailing, cross):
    m, n = trailing.shape
    fq = cross.shape[0]
    nb = n // B
    h = m // K2
    npl = 1 + h
    f32 = jnp.float32
    anywhere = pl.BlockSpec(memory_space=pl.ANY)
    vmem = pl.BlockSpec(memory_space=pltpu.VMEM)
    dma = pltpu.SemaphoreType.DMA
    pan, q, linv, ans, tq = pl.pallas_call(
        functools.partial(exchange, R, C),
        out_shape=(
            jax.ShapeDtypeStruct((2, 2, B + m // 2, B), f32),
            jax.ShapeDtypeStruct((K2, n), f32),
            jax.ShapeDtypeStruct((K2, K2), f32),
            jax.ShapeDtypeStruct((fq * C, n), f32),
            jax.ShapeDtypeStruct((fq * C, K2), f32),
        ),
        in_specs=[anywhere, anywhere],
        out_specs=(anywhere, anywhere, vmem, anywhere, anywhere),
        scratch_shapes=[
            pltpu.VMEM((K2, K2), f32),
            pltpu.VMEM((H, 2 * H), f32),
            dma((2, nb)), dma((nb,)), dma((2, nb)),
            dma((2, npl)), dma((2, npl)), dma((2, npl)), dma((2, npl)),
            dma((5 + nb,)),
            dma((C, nb)), dma((C, nb)), dma((C,)), dma((C,)),
        ],
        compiler_params=pltpu.CompilerParams(
            collective_id=0, has_side_effects=True, vmem_limit_bytes=32 * 1024 * 1024
        ),
        cost_estimate=pl.CostEstimate(flops=10**9, bytes_accessed=32 * 10**6, transcendentals=0),
        name="exchange",
    )(trailing, cross)

    def whole(shape):
        return pl.BlockSpec(shape, lambda i: (0,) * len(shape))

    return pl.pallas_call(
        functools.partial(update, R, C),
        grid=(m // B,),
        out_shape=(jax.ShapeDtypeStruct((m, n), f32), jax.ShapeDtypeStruct((fq * C, n), f32)),
        in_specs=[
            pl.BlockSpec((2, 1, B, B), lambda i: (0, i // h, 1 + i % h, 0)),
            whole((K2, n)),
            whole((K2, K2)),
            pl.BlockSpec((B, n), lambda i: (i, 0)),
            whole((fq * C, n)),
            whole((fq * C, K2)),
        ],
        out_specs=(pl.BlockSpec((B, n), lambda i: (i, 0)), whole((fq * C, n))),
        scratch_shapes=[pltpu.VMEM((K2, n), jnp.bfloat16), pltpu.VMEM((K2, n), jnp.bfloat16)],
        compiler_params=pltpu.CompilerParams(
            dimension_semantics=("arbitrary",), vmem_limit_bytes=52 * 1024 * 1024
        ),
        cost_estimate=pl.CostEstimate(flops=2 * m * n * K2 * 3, bytes_accessed=8 * m * n, transcendentals=0),
        name="update",
    )(pan, q, linv, trailing, ans, tq)


def solution(mesh):
    return jax.shard_map(
        functools.partial(on_device, mesh.shape["row"], mesh.shape["col"]),
        mesh=mesh,
        in_specs=(P("row", "col"), P(("row", "col"), None)),
        out_specs=(P("row", "col"), P("row", "col")),
        check_vma=False,
    )
```
